128 devices in a mesh: row: 16 (over x_hi, z, core), col: 8 (over x_lo, y).
Axes of the slice: x: 4 (x_hi: 2, x_lo: 2; x = x_hi * 2 + x_lo), y: 4, z: 4, core: 2. Of those that a mesh axis runs over, the one named last changes fastest.
Arguments:
- pair: bfloat16 [1024, 1024, 128], P('row', 'col'), may hold values from -6 to 6
- in_gain: float32 [128], replicated, may hold values from 0.25 to 1.75
- in_bias: float32 [128], replicated, may hold values from -3 to 3
- w_proj: bfloat16 [128, 128], replicated, may hold values from -0.5 to 0.5
- w_gate: bfloat16 [128, 128], replicated, may hold values from -0.5 to 0.5
- w_out_gate: bfloat16 [128, 128], replicated, may hold values from -0.5 to 0.5
- out_gain: float32 [64], replicated, may hold values from 0.25 to 1.75
- out_bias: float32 [64], replicated, may hold values from -3 to 3
- w_out: bfloat16 [64, 128], replicated, may hold values from -0.75 to 0.75
Outputs:
- update: bfloat16 [1024, 1024, 128], P('row', 'col')
The draws below stay inside these ranges and needn't reach their ends.
All inputs are finite; a program needn't handle non-finite values.
Results may differ from the reference program's by a relative error of at most 0.018.
Values may be sent and summed in bfloat16 or wider, within the bound.
No kernel may reach another device: no remote copies, remote signals or barrier semaphores. Data moves between devices by JAX's collectives and lax.ppermute only.
A program may use at most 128 MiB of HBM per device.

```python
import jax
import jax.numpy as jnp
from jax import lax

PAIR_C = 128
HIDDEN_C = 64
RESIDUES = 1024


def block_levels(rng, extent, shards, smallest, top_value):
    loudness = 1.0
    for position, blocks in shards:
        steps = jax.random.uniform(jax.random.fold_in(jax.random.fold_in(rng, 6), position), (blocks,), jnp.float32, smallest / len(shards), top_value / len(shards))
        loudness = loudness * jnp.repeat(jnp.exp(steps), extent[position] // blocks).reshape((-1,) + (1,) * (len(extent) - 1 - position))
    return loudness


def centred(rng, extent, scale, most, cuts=(), kind=jnp.bfloat16):
    drawn = jax.random.normal(rng, extent, jnp.float32) * scale
    if len(cuts) > 0:
        drawn = block_levels(rng, extent, cuts, -0.22, 0.18) * drawn
    return jnp.clip(drawn, min=-most, max=most).astype(kind)


def setup_inputs(seed: int = 0) -> dict:
    arg_keys = jax.random.split(jax.random.key(seed), 10)
    pair = centred(arg_keys[0], (RESIDUES, RESIDUES, PAIR_C), 1.0, 6.0, ((0, 16), (1, 8)))
    in_gain = jnp.clip(1.0 + 0.15 * jax.random.normal(arg_keys[1], (PAIR_C,), jnp.float32), 0.25, 1.75)
    in_bias = centred(arg_keys[2], (PAIR_C,), 0.5, 3.0, (), jnp.float32)
    w_proj = centred(arg_keys[3], (PAIR_C, 2 * HIDDEN_C), PAIR_C ** -0.5, 0.5)
    w_gate = centred(arg_keys[4], (PAIR_C, 2 * HIDDEN_C), PAIR_C ** -0.5, 0.5)
    w_out_gate = centred(arg_keys[5], (PAIR_C, PAIR_C), PAIR_C ** -0.5, 0.5)
    out_gain = jnp.clip(1.0 + 0.15 * jax.random.normal(arg_keys[6], (HIDDEN_C,), jnp.float32), 0.25, 1.75)
    out_bias = centred(arg_keys[7], (HIDDEN_C,), 0.5, 3.0, (), jnp.float32)
    w_out = centred(arg_keys[8], (HIDDEN_C, PAIR_C), HIDDEN_C ** -0.5, 0.75)
    return {"pair": pair, "in_gain": in_gain, "in_bias": in_bias, "w_proj": w_proj, "w_gate": w_gate, "w_out_gate": w_out_gate, "out_gain": out_gain, "out_bias": out_bias, "w_out": w_out}


def normalize(values, gain, bias):
    mean = lax.optimization_barrier(jnp.mean(values, axis=-1, keepdims=True))
    centered = values - mean
    var = lax.optimization_barrier(jnp.mean(centered * centered, axis=-1, keepdims=True))
    return centered / jnp.sqrt(var + 1e-05) * gain + bias

def reference(pair, in_gain, in_bias, w_proj, w_gate, w_out_gate, out_gain, out_bias, w_out):
    normed = normalize(pair.astype(jnp.float32), in_gain, in_bias).astype(jnp.bfloat16)
    flat = normed.reshape(-1, PAIR_C)
    proj = jnp.dot(flat, w_proj, preferred_element_type=jnp.float32)
    gates = jnp.dot(flat, w_gate, preferred_element_type=jnp.float32)
    both = (jax.nn.sigmoid(gates) * proj).astype(jnp.bfloat16).reshape(RESIDUES, RESIDUES, 2 * HIDDEN_C)
    a_side = jnp.transpose(both[:, :, :HIDDEN_C], (2, 0, 1)).astype(jnp.float32)
    b_side = jnp.transpose(both[:, :, HIDDEN_C:], (2, 0, 1)).astype(jnp.float32)
    mixed = jnp.matmul(a_side, jnp.swapaxes(b_side, 1, 2))
    mixed = jnp.transpose(mixed, (1, 2, 0))
    mixed_normed = normalize(mixed, out_gain, out_bias).astype(jnp.bfloat16)
    projected = jnp.dot(mixed_normed.reshape(-1, HIDDEN_C), w_out, preferred_element_type=jnp.float32)
    out_gates = jax.nn.sigmoid(jnp.dot(flat, w_out_gate, preferred_element_type=jnp.float32))
    update = (out_gates * projected).astype(jnp.bfloat16)
    return update.reshape(RESIDUES, RESIDUES, PAIR_C)
```

```python
import jax
import jax.numpy as jnp
from jax import lax
from jax.sharding import Mesh
from jax.sharding import PartitionSpec as P

CHIPS = ("xh", "z", "xl", "y")


def normalize(values, gain, bias):
    mean = jnp.mean(values, axis=-1, keepdims=True)
    centered = values - mean
    var = jnp.mean(centered * centered, axis=-1, keepdims=True)
    return centered * lax.rsqrt(var + 1e-05) * gain + bias


def local(pair, in_gain, in_bias, w_proj, w_gate, w_out_gate, out_gain, out_bias, w_out):
    rows, cols, channels = pair.shape
    hidden = w_out.shape[0]
    normed = normalize(pair.astype(jnp.float32), in_gain, in_bias).astype(jnp.bfloat16)
    flat = normed.reshape(-1, channels)
    proj = jnp.dot(flat, w_proj, preferred_element_type=jnp.float32)
    gates = jnp.dot(flat, w_gate, preferred_element_type=jnp.float32)
    both = (jax.nn.sigmoid(gates) * proj).astype(jnp.bfloat16).reshape(rows, cols, 2, hidden)
    lead = jnp.transpose(both, (3, 2, 0, 1))
    chan = lax.all_to_all(lead, CHIPS, 0, 0, tiled=True)
    chan = chan.reshape(2, 4, 2, 4, 2, rows, cols)
    mine = jnp.transpose(chan, (4, 0, 1, 5, 2, 3, 6)).reshape(2, 8 * rows, 8 * cols)
    a_half, b_half = mine[0], mine[1]
    b_other = lax.ppermute(b_half, "core", [(0, 1), (1, 0)])
    core = lax.axis_index("core")
    own = lax.dot_general(a_half, b_half, (((1,), (1,)), ((), ())), preferred_element_type=jnp.float32)
    oth = lax.dot_general(a_half, b_other, (((1,), (1,)), ((), ())), preferred_element_type=jnp.float32)
    own = own.astype(jnp.bfloat16).reshape(2, 4, rows, 2, 4, rows)
    oth = oth.astype(jnp.bfloat16).reshape(2, 4, rows, 2, 4, rows)
    first = jnp.where(core == 0, own, oth)
    second = jnp.where(core == 0, oth, own)
    full = jnp.stack([first, second], axis=5).reshape(2, 4, rows, 2, 4, cols)
    full = jnp.transpose(full, (0, 1, 3, 4, 2, 5)).reshape(64, rows, cols)
    back = lax.all_to_all(full, CHIPS, 0, 0, tiled=True)
    mixed = jnp.transpose(back, (1, 2, 0)).astype(jnp.float32)
    mixed_normed = normalize(mixed, out_gain, out_bias).astype(jnp.bfloat16)
    projected = jnp.dot(mixed_normed.reshape(-1, hidden), w_out, preferred_element_type=jnp.float32)
    out_gates = jax.nn.sigmoid(jnp.dot(flat, w_out_gate, preferred_element_type=jnp.float32))
    update = (out_gates * projected).astype(jnp.bfloat16)
    return update.reshape(rows, cols, channels)


def solution(mesh):
    fine = Mesh(mesh.devices.reshape(2, 4, 2, 2, 4), ("xh", "z", "core", "xl", "y"))
    place = P(("xh", "z", "core"), ("xl", "y"), None)
    return jax.shard_map(
        local,
        mesh=fine,
        in_specs=(place, P(), P(), P(), P(), P(), P(), P(), P()),
        out_specs=place,
        check_vma=False,
    )
```

```python
import jax
import jax.numpy as jnp
from jax import lax
from jax.experimental import pallas as pl
from jax.experimental.pallas import tpu as pltpu
from jax.sharding import Mesh
from jax.sharding import PartitionSpec as P

CHIPS = ("xh", "z", "xl", "y")
STEP = 16
EPS = 1e-05
VMEM = 48 << 20
NT = (((1,), (1,)), ((), ()))
TN = (((0,), (0,)), ((), ()))


def sigmoid(x):
    return 0.5 * jnp.tanh(0.5 * x) + 0.5


def normalized(x, gain, bias):
    mean = jnp.mean(x, axis=-1, keepdims=True)
    centered = x - mean
    var = jnp.mean(centered * centered, axis=-1, keepdims=True)
    return (centered * lax.rsqrt(var + EPS) * gain + bias).astype(jnp.bfloat16)


def pre_kernel(pair, gain, bias, w_proj, w_gate, out, weights, held):
    channels = pair.shape[2]
    hidden = channels // 2

    @pl.when(pl.program_id(0) == 0)
    def _():
        weights[:channels] = w_proj[...].T
        weights[channels:] = w_gate[...].T

    for t in range(0, STEP, 2):
        x = pair[t : t + 2].reshape(2 * pair.shape[1], channels).astype(jnp.float32)
        normed = normalized(x, gain[...], bias[...])
        both = lax.dot_general(weights[...], normed, NT, preferred_element_type=jnp.float32)
        y = sigmoid(both[channels:]) * both[:channels]
        held[t] = y[:, : pair.shape[1]]
        held[t + 1] = y[:, pair.shape[1] :]
    for c in range(channels):
        out[c % hidden, c // hidden] = held[:, c, :].astype(jnp.bfloat16)


def pre(pair, gain, bias, w_proj, w_gate):
    rows, cols, channels = pair.shape
    hidden = channels // 2
    whole = lambda *shape: pl.BlockSpec(shape, lambda i: (0,) * len(shape))
    return pl.pallas_call(
        pre_kernel,
        grid=(rows // STEP,),
        in_specs=[
            pl.BlockSpec((STEP, cols, channels), lambda i: (i, 0, 0)),
            whole(1, channels),
            whole(1, channels),
            whole(channels, channels),
            whole(channels, channels),
        ],
        out_specs=pl.BlockSpec((hidden, 2, STEP, cols), lambda i: (0, 0, i, 0)),
        out_shape=jax.ShapeDtypeStruct((hidden, 2, rows, cols), jnp.bfloat16),
        scratch_shapes=[
            pltpu.VMEM((2 * channels, channels), jnp.bfloat16),
            pltpu.VMEM((STEP, channels, cols), jnp.float32),
        ],
        compiler_params=pltpu.CompilerParams(vmem_limit_bytes=VMEM),
        cost_estimate=pl.CostEstimate(flops=1 << 30, bytes_accessed=4 << 20, transcendentals=1 << 20),
        name="pre",
    )(pair, gain, bias, w_proj, w_gate)


def gate_kernel(pair, gain, bias, w_out_gate, out):
    channels = pair.shape[2]
    for t in range(0, STEP, 2):
        x = pair[t : t + 2].reshape(2 * pair.shape[1], channels).astype(jnp.float32)
        normed = normalized(x, gain[...], bias[...])
        gates = jnp.dot(normed, w_out_gate[...], preferred_element_type=jnp.float32)
        out[t : t + 2] = sigmoid(gates).astype(jnp.bfloat16).reshape(2, pair.shape[1], channels)


def gate(pair, gain, bias, w_out_gate):
    rows, cols, channels = pair.shape
    whole = lambda *shape: pl.BlockSpec(shape, lambda i: (0,) * len(shape))
    block = pl.BlockSpec((STEP, cols, channels), lambda i: (i, 0, 0))
    return pl.pallas_call(
        gate_kernel,
        grid=(rows // STEP,),
        in_specs=[block, whole(1, channels), whole(1, channels), whole(channels, channels)],
        out_specs=block,
        out_shape=jax.ShapeDtypeStruct((rows, cols, channels), jnp.bfloat16),
        compiler_params=pltpu.CompilerParams(vmem_limit_bytes=VMEM),
        cost_estimate=pl.CostEstimate(flops=1 << 30, bytes_accessed=16 << 20, transcendentals=1 << 20),
        name="gate",
    )(pair, gain, bias, w_out_gate)


def mid_kernel(core, chan, other, out, a_side, b_side):
    groups, rows, cols = other.shape
    across = 8
    mine = pl.multiple_of(core[0] * rows, rows)
    theirs = pl.multiple_of(rows - core[0] * rows, rows)
    for s in range(groups):
        r, q = s // across, s % across
        here = slice(q * cols, (q + 1) * cols)
        a_side[r * rows : (r + 1) * rows, here] = chan[s, 0]
        b_side[r, pl.ds(mine, rows), here] = chan[s, 1]
        b_side[r, pl.ds(theirs, rows), here] = other[s]
    for g in range(0, across, 2):
        b = b_side[g : g + 2].reshape(2 * cols, across * cols)
        m = lax.dot_general(a_side[...], b, NT, preferred_element_type=jnp.float32).astype(jnp.bfloat16)
        for r in range(groups // across):
            for h in range(2):
                out[r * across + g + h] = m[r * rows : (r + 1) * rows, h * cols : (h + 1) * cols]


def mid(core, chan, other):
    groups, rows, cols = other.shape
    return pl.pallas_call(
        mid_kernel,
        in_specs=[
            pl.BlockSpec(memory_space=pltpu.SMEM),
            pl.BlockSpec(memory_space=pltpu.VMEM),
            pl.BlockSpec(memory_space=pltpu.VMEM),
        ],
        out_specs=pl.BlockSpec(memory_space=pltpu.VMEM),
        out_shape=jax.ShapeDtypeStruct((groups, rows, cols), jnp.bfloat16),
        scratch_shapes=[
            pltpu.VMEM((8 * rows, 8 * cols), jnp.bfloat16),
            pltpu.VMEM((8, 2 * rows, 8 * cols), jnp.bfloat16),
        ],
        compiler_params=pltpu.CompilerParams(vmem_limit_bytes=VMEM),
        cost_estimate=pl.CostEstimate(flops=1 << 30, bytes_accessed=4 << 20, transcendentals=0),
        name="mid",
    )(core, chan, other)


def post_kernel(back, gates, gain, bias, w_out, out, held):
    hidden = back.shape[0]
    m = back[...].astype(jnp.float32)
    mean = jnp.mean(m, axis=0, keepdims=True)
    centered = m - mean
    var = jnp.mean(centered * centered, axis=0, keepdims=True)
    scale = lax.rsqrt(var + EPS)
    for c in range(hidden):
        held[c] = centered[c] * scale[0] * gain[c] + bias[c]
    for t in range(STEP):
        normed = held[:, t, :].astype(jnp.bfloat16)
        projected = lax.dot_general(normed, w_out[...], TN, preferred_element_type=jnp.float32)
        out[t] = (gates[t].astype(jnp.float32) * projected).astype(jnp.bfloat16)


def post(back, gates, gain, bias, w_out):
    hidden, rows, cols = back.shape
    channels = w_out.shape[1]
    block = pl.BlockSpec((STEP, cols, channels), lambda i: (i, 0, 0))
    return pl.pallas_call(
        post_kernel,
        grid=(rows // STEP,),
        in_specs=[
            pl.BlockSpec((hidden, STEP, cols), lambda i: (0, i, 0)),
            block,
            pl.BlockSpec(memory_space=pltpu.SMEM),
            pl.BlockSpec(memory_space=pltpu.SMEM),
            pl.BlockSpec((hidden, channels), lambda i: (0, 0)),
        ],
        out_specs=block,
        out_shape=jax.ShapeDtypeStruct((rows, cols, channels), jnp.bfloat16),
        scratch_shapes=[pltpu.VMEM((hidden, STEP, cols), jnp.float32)],
        compiler_params=pltpu.CompilerParams(vmem_limit_bytes=VMEM),
        cost_estimate=pl.CostEstimate(flops=1 << 28, bytes_accessed=5 << 20, transcendentals=0),
        name="post",
    )(back, gates, gain, bias, w_out)


def local(pair, in_gain, in_bias, w_proj, w_gate, w_out_gate, out_gain, out_bias, w_out):
    gain, bias = in_gain.reshape(1, -1), in_bias.reshape(1, -1)
    lead = pre(pair, gain, bias, w_proj, w_gate)
    gates = gate(pair, gain, bias, w_out_gate)
    chan = lax.all_to_all(lead, CHIPS, 0, 0, tiled=True)
    other = lax.ppermute(chan[:, 1], "core", [(0, 1), (1, 0)])
    core = lax.axis_index("core").astype(jnp.int32).reshape(1)
    back = lax.all_to_all(mid(core, chan, other), CHIPS, 0, 0, tiled=True)
    return post(back, gates, out_gain, out_bias, w_out)


def solution(mesh):
    fine = Mesh(mesh.devices.reshape(2, 4, 2, 2, 4), ("xh", "z", "core", "xl", "y"))
    place = P(("xh", "z", "core"), ("xl", "y"), None)
    return jax.shard_map(
        local,
        mesh=fine,
        in_specs=(place, P(), P(), P(), P(), P(), P(), P(), P()),
        out_specs=place,
        check_vma=False,
    )
```

```python
import jax
import jax.numpy as jnp
from jax import lax
from jax.experimental import pallas as pl
from jax.experimental.pallas import tpu as pltpu
from jax.sharding import Mesh
from jax.sharding import PartitionSpec as P

CHIPS = ("xh", "z", "xl", "y")
STEP = 16
EPS = 1e-05
FEW = 24 << 20
VMEM = 48 << 20
NEARLY = 60 << 20
MOST = 58 << 20
NT = (((1,), (1,)), ((), ()))
TN = (((0,), (0,)), ((), ()))


def sigmoid(x):
    return 0.5 * jnp.tanh(0.5 * x) + 0.5


def normalized(x, gain, bias):
    share = 1.0 / x.shape[-1]
    centered = x - jnp.sum(x, axis=-1, keepdims=True) * share
    var = jnp.sum(centered * centered, axis=-1, keepdims=True) * share
    return (centered * lax.rsqrt(var + EPS) * gain + bias).astype(jnp.bfloat16)


def copies(pairs, sems):
    return [pltpu.make_async_copy(src, dst, sems.at[n]) for n, (src, dst) in enumerate(pairs)]


def chunks(source, target, sems):
    rows = target.shape[0]
    spans = [slice(s, s + STEP) for s in range(0, rows, STEP)]
    return copies([(source.at[span], target.at[span]) for span in spans], sems)


def pre_kernel(pair, gain, bias, w_proj, w_gate, out, held, made, affine, loaded, weights, gains, biases, sems, held_sems, out_sems):
    rows, cols, channels = held.shape
    hidden = channels // 2
    small = copies(
        [(gain, affine.at[0:1]), (bias, affine.at[1:2]), (w_proj, loaded.at[0]), (w_gate, loaded.at[1])], sems
    )
    large = chunks(pair, held, held_sems)
    for copy in small + large:
        copy.start()
    for copy in small:
        copy.wait()
    weights[:channels] = loaded[0].T
    weights[channels:] = loaded[1].T
    gains[...] = jnp.broadcast_to(affine[0:1], (cols, channels)).T
    biases[...] = jnp.broadcast_to(affine[1:2], (cols, channels)).T

    def products(first):
        x = held[first : first + 2].reshape(2 * cols, channels).T.astype(jnp.float32)
        centered = x - jnp.sum(x, axis=0, keepdims=True) * (1.0 / channels)
        var = jnp.sum(centered * centered, axis=0, keepdims=True) * (1.0 / channels)
        x = centered * lax.rsqrt(var + EPS)
        normed = [x[:, h * cols : (h + 1) * cols] * gains[...] + biases[...] for h in range(2)]
        normed = jnp.concatenate(normed, axis=1).astype(jnp.bfloat16)
        both = jnp.dot(weights[...], normed, preferred_element_type=jnp.float32)
        return (sigmoid(both[channels:]) * both[:channels]).astype(jnp.bfloat16)

    spans = [slice(s, s + STEP) for s in range(0, rows, STEP)]
    writes = copies([(made.at[:, :, span], out.at[:, :, span]) for span in spans], out_sems)
    for s in range(0, rows, STEP):
        large[s // STEP].wait()
        y = [products(s + t) for t in range(0, STEP, 2)]
        for c in range(0, channels, 16):
            lead = jnp.stack([v[c : c + 16, h * cols : (h + 1) * cols] for v in y for h in range(2)], axis=0)
            made[c % hidden : c % hidden + 16, c // hidden, s : s + STEP] = jnp.swapaxes(lead, 0, 1)
        writes[s // STEP].start()
    for copy in writes:
        copy.wait()


def pre(pair, gain, bias, w_proj, w_gate):
    rows, cols, channels = pair.shape
    hidden = channels // 2
    return pl.pallas_call(
        pre_kernel,
        in_specs=[pl.BlockSpec(memory_space=pl.ANY)] * 5,
        out_specs=pl.BlockSpec(memory_space=pl.ANY),
        out_shape=jax.ShapeDtypeStruct((hidden, 2, rows, cols), jnp.bfloat16),
        scratch_shapes=[
            pltpu.VMEM((rows, cols, channels), jnp.bfloat16),
            pltpu.VMEM((hidden, 2, rows, cols), jnp.bfloat16),
            pltpu.VMEM((2, channels), jnp.float32),
            pltpu.VMEM((2, channels, channels), jnp.bfloat16),
            pltpu.VMEM((2 * channels, channels), jnp.bfloat16),
            pltpu.VMEM((channels, cols), jnp.float32),
            pltpu.VMEM((channels, cols), jnp.float32),
            pltpu.SemaphoreType.DMA((4,)),
            pltpu.SemaphoreType.DMA((rows // STEP,)),
            pltpu.SemaphoreType.DMA((rows // STEP,)),
        ],
        compiler_params=pltpu.CompilerParams(vmem_limit_bytes=MOST),
        cost_estimate=pl.CostEstimate(flops=1 << 30, bytes_accessed=4 << 20, transcendentals=1 << 20),
        name="pre",
    )(pair, gain, bias, w_proj, w_gate)


def gate_kernel(pair, gain, bias, w_out_gate, out, held, affine, loaded, sems, held_sems):
    rows, cols, channels = held.shape
    small = copies([(gain, affine.at[0:1]), (bias, affine.at[1:2]), (w_out_gate, loaded)], sems)
    large = chunks(pair, held, held_sems)
    for copy in small + large:
        copy.start()
    for copy in small:
        copy.wait()
    for s in range(0, rows, STEP):
        large[s // STEP].wait()
        for t in range(s, s + STEP, 2):
            x = held[t : t + 2].reshape(2 * cols, channels).astype(jnp.float32)
            normed = normalized(x, affine[0:1], affine[1:2])
            gates = jnp.dot(normed, loaded[...], preferred_element_type=jnp.float32)
            out[t : t + 2] = sigmoid(gates).astype(jnp.bfloat16).reshape(2, cols, channels)


def gate(pair, gain, bias, w_out_gate):
    rows, cols, channels = pair.shape
    return pl.pallas_call(
        gate_kernel,
        in_specs=[pl.BlockSpec(memory_space=pl.ANY)] * 4,
        out_specs=pl.BlockSpec(memory_space=pltpu.VMEM),
        out_shape=jax.ShapeDtypeStruct((rows, cols, channels), jnp.bfloat16),
        scratch_shapes=[
            pltpu.VMEM((rows, cols, channels), jnp.bfloat16),
            pltpu.VMEM((2, channels), jnp.float32),
            pltpu.VMEM((channels, channels), jnp.bfloat16),
            pltpu.SemaphoreType.DMA((3,)),
            pltpu.SemaphoreType.DMA((rows // STEP,)),
        ],
        compiler_params=pltpu.CompilerParams(vmem_limit_bytes=NEARLY),
        cost_estimate=pl.CostEstimate(flops=1 << 30, bytes_accessed=16 << 20, transcendentals=1 << 20),
        name="gate",
    )(pair, gain, bias, w_out_gate)


def mid_kernel(core, chan, other, out, a_side, b_side):
    groups, rows, cols = other.shape
    across = 8
    mine = pl.multiple_of(core[0] * rows, rows)
    theirs = pl.multiple_of(rows - core[0] * rows, rows)
    for s in range(groups):
        r, q = s // across, s % across
        here = slice(q * cols, (q + 1) * cols)
        a_side[r * rows : (r + 1) * rows, here] = chan[s, 0]
        b_side[r, pl.ds(mine, rows), here] = chan[s, 1]
        b_side[r, pl.ds(theirs, rows), here] = other[s]
    for g in range(0, across, 2):
        b = b_side[g : g + 2].reshape(2 * cols, across * cols)
        m = lax.dot_general(a_side[...], b, NT, preferred_element_type=jnp.float32).astype(jnp.bfloat16)
        for r in range(groups // across):
            for h in range(2):
                out[r * across + g + h] = m[r * rows : (r + 1) * rows, h * cols : (h + 1) * cols]


def mid(core, chan, other):
    groups, rows, cols = other.shape
    return pl.pallas_call(
        mid_kernel,
        in_specs=[
            pl.BlockSpec(memory_space=pltpu.SMEM),
            pl.BlockSpec(memory_space=pltpu.VMEM),
            pl.BlockSpec(memory_space=pltpu.VMEM),
        ],
        out_specs=pl.BlockSpec(memory_space=pltpu.VMEM),
        out_shape=jax.ShapeDtypeStruct((groups, rows, cols), jnp.bfloat16),
        scratch_shapes=[
            pltpu.VMEM((8 * rows, 8 * cols), jnp.bfloat16),
            pltpu.VMEM((8, 2 * rows, 8 * cols), jnp.bfloat16),
        ],
        compiler_params=pltpu.CompilerParams(vmem_limit_bytes=VMEM),
        cost_estimate=pl.CostEstimate(flops=1 << 30, bytes_accessed=4 << 20, transcendentals=0),
        name="mid",
    )(core, chan, other)


def post_kernel(back, gates, gain, bias, w_out, out, made, loaded, wide, sem, out_sems):
    hidden, rows, cols = back.shape
    channels = loaded.shape[1]
    weight = pltpu.make_async_copy(w_out, loaded, sem)
    weight.start()
    wide[...] = jnp.zeros_like(wide)
    weight.wait()
    wide[:hidden, :channels] = loaded[...]
    wide[hidden:, channels:] = loaded[...]
    writes = chunks(made, out, out_sems)
    for s in range(0, rows, STEP):
        m = back[:, s : s + STEP, :].astype(jnp.float32)
        centered = m - jnp.sum(m, axis=0) * (1.0 / hidden)
        scale = lax.rsqrt(jnp.sum(centered * centered, axis=0) * (1.0 / hidden) + EPS)
        turned = []
        for c in range(0, hidden, 8):
            lead = jnp.stack([centered[c + d] * scale * gain[c + d] + bias[c + d] for d in range(8)], axis=0)
            turned.append(jnp.swapaxes(lead, 0, 1))
        normed = jnp.concatenate(turned, axis=1).astype(jnp.bfloat16)
        for t in range(0, STEP, 2):
            two = normed[t : t + 2].reshape(2 * hidden, cols)
            projected = lax.dot_general(two, wide[...], TN, preferred_element_type=jnp.float32)
            for h in range(2):
                mine = projected[:, h * channels : (h + 1) * channels]
                made[s + t + h] = (gates[s + t + h].astype(jnp.float32) * mine).astype(jnp.bfloat16)
        writes[s // STEP].start()
    for copy in writes:
        copy.wait()


def post(back, gates, gain, bias, w_out):
    hidden, rows, cols = back.shape
    channels = w_out.shape[1]
    whole = pl.BlockSpec(memory_space=pl.ANY)
    scalars = pl.BlockSpec(memory_space=pltpu.SMEM)
    return pl.pallas_call(
        post_kernel,
        in_specs=[pl.BlockSpec(memory_space=pltpu.VMEM)] * 2 + [scalars, scalars, whole],
        out_specs=whole,
        out_shape=jax.ShapeDtypeStruct((rows, cols, channels), jnp.bfloat16),
        scratch_shapes=[
            pltpu.VMEM((rows, cols, channels), jnp.bfloat16),
            pltpu.VMEM((hidden, channels), jnp.bfloat16),
            pltpu.VMEM((2 * hidden, 2 * channels), jnp.bfloat16),
            pltpu.SemaphoreType.DMA,
            pltpu.SemaphoreType.DMA((rows // STEP,)),
        ],
        compiler_params=pltpu.CompilerParams(vmem_limit_bytes=FEW),
        cost_estimate=pl.CostEstimate(flops=1 << 28, bytes_accessed=5 << 20, transcendentals=0),
        name="post",
    )(back, gates, gain, bias, w_out)


def local(pair, in_gain, in_bias, w_proj, w_gate, w_out_gate, out_gain, out_bias, w_out):
    gain, bias = in_gain.reshape(1, -1), in_bias.reshape(1, -1)
    lead = pre(pair, gain, bias, w_proj, w_gate)
    gates = gate(pair, gain, bias, w_out_gate)
    chan = lax.all_to_all(lead, CHIPS, 0, 0, tiled=True)
    chan, gates = lax.optimization_barrier((chan, gates))
    other = lax.ppermute(chan[:, 1], "core", [(0, 1), (1, 0)])
    core = lax.axis_index("core").astype(jnp.int32).reshape(1)
    back = lax.all_to_all(mid(core, chan, other), CHIPS, 0, 0, tiled=True)
    return post(back, gates, out_gain, out_bias, w_out)


def solution(mesh):
    fine = Mesh(mesh.devices.reshape(2, 4, 2, 2, 4), ("xh", "z", "core", "xl", "y"))
    place = P(("xh", "z", "core"), ("xl", "y"), None)
    return jax.shard_map(
        local,
        mesh=fine,
        in_specs=(place, P(), P(), P(), P(), P(), P(), P(), P()),
        out_specs=place,
        check_vma=False,
    )
```

```python
import jax
import jax.numpy as jnp
from jax import lax
from jax.experimental import pallas as pl
from jax.experimental.pallas import tpu as pltpu
from jax.sharding import Mesh
from jax.sharding import PartitionSpec as P

CHIPS = ("xh", "z", "y", "xl")
PLACES = [(xh * 4 + z, xl * 4 + y) for xh in range(2) for z in range(4) for y in range(4) for xl in range(2)]
STEP = 16
EPS = 1e-05
FEW = 24 << 20
VMEM = 48 << 20
NEARLY = 60 << 20
MOST = 58 << 20
NT = (((1,), (1,)), ((), ()))
TN = (((0,), (0,)), ((), ()))


def sigmoid(x):
    return 0.5 * jnp.tanh(0.5 * x) + 0.5


def normalized(x, gain, bias):
    share = 1.0 / x.shape[-1]
    centered = x - jnp.sum(x, axis=-1, keepdims=True) * share
    var = jnp.sum(centered * centered, axis=-1, keepdims=True) * share
    return (centered * lax.rsqrt(var + EPS) * gain + bias).astype(jnp.bfloat16)


def copies(pairs, sems):
    return [pltpu.make_async_copy(src, dst, sems.at[n]) for n, (src, dst) in enumerate(pairs)]


def chunks(source, target, sems):
    rows = target.shape[0]
    spans = [slice(s, s + STEP) for s in range(0, rows, STEP)]
    return copies([(source.at[span], target.at[span]) for span in spans], sems)


def pre_kernel(pair, gain, bias, w_proj, w_gate, out, held, made, affine, loaded, weights, gains, biases, sems, held_sems, out_sems):
    rows, cols, channels = held.shape
    hidden = channels // 2
    small = copies(
        [(gain, affine.at[0:1]), (bias, affine.at[1:2]), (w_proj, loaded.at[0]), (w_gate, loaded.at[1])], sems
    )
    large = chunks(pair, held, held_sems)
    for copy in small + large:
        copy.start()
    for copy in small:
        copy.wait()
    for n in range(2):
        half = loaded[n].astype(jnp.float32).T * 0.5
        weights[n * channels : (n + 1) * channels] = half.astype(jnp.bfloat16)
    gains[...] = jnp.broadcast_to(affine[0:1], (cols, channels)).T
    biases[...] = jnp.broadcast_to(affine[1:2], (cols, channels)).T

    def products(first):
        x = held[first : first + 2].reshape(2 * cols, channels).T.astype(jnp.float32)
        centered = x - jnp.sum(x, axis=0, keepdims=True) * (1.0 / channels)
        var = jnp.sum(centered * centered, axis=0, keepdims=True) * (1.0 / channels)
        x = centered * lax.rsqrt(var + EPS)
        normed = [x[:, h * cols : (h + 1) * cols] * gains[...] + biases[...] for h in range(2)]
        normed = jnp.concatenate(normed, axis=1).astype(jnp.bfloat16)
        both = jnp.dot(weights[...], normed, preferred_element_type=jnp.float32)
        return (jnp.tanh(both[channels:]) * both[:channels] + both[:channels]).astype(jnp.bfloat16)

    spans = [slice(s, s + STEP) for s in range(0, rows, STEP)]
    writes = copies([(made.at[:, :, span], out.at[:, :, span]) for span in spans], out_sems)
    for s in range(0, rows, STEP):
        large[s // STEP].wait()
        y = [products(s + t) for t in range(0, STEP, 2)]
        for c in range(0, channels, 16):
            lead = jnp.stack([v[c : c + 16, h * cols : (h + 1) * cols] for v in y for h in range(2)], axis=0)
            made[c % hidden : c % hidden + 16, c // hidden, s : s + STEP] = jnp.swapaxes(lead, 0, 1)
        writes[s // STEP].start()
    for copy in writes:
        copy.wait()


def pre(pair, gain, bias, w_proj, w_gate):
    rows, cols, channels = pair.shape
    hidden = channels // 2
    return pl.pallas_call(
        pre_kernel,
        in_specs=[pl.BlockSpec(memory_space=pl.ANY)] * 5,
        out_specs=pl.BlockSpec(memory_space=pl.ANY),
        out_shape=jax.ShapeDtypeStruct((hidden, 2, rows, cols), jnp.bfloat16),
        scratch_shapes=[
            pltpu.VMEM((rows, cols, channels), jnp.bfloat16),
            pltpu.VMEM((hidden, 2, rows, cols), jnp.bfloat16),
            pltpu.VMEM((2, channels), jnp.float32),
            pltpu.VMEM((2, channels, channels), jnp.bfloat16),
            pltpu.VMEM((2 * channels, channels), jnp.bfloat16),
            pltpu.VMEM((channels, cols), jnp.float32),
            pltpu.VMEM((channels, cols), jnp.float32),
            pltpu.SemaphoreType.DMA((4,)),
            pltpu.SemaphoreType.DMA((rows // STEP,)),
            pltpu.SemaphoreType.DMA((rows // STEP,)),
        ],
        compiler_params=pltpu.CompilerParams(vmem_limit_bytes=MOST),
        cost_estimate=pl.CostEstimate(flops=1 << 30, bytes_accessed=4 << 20, transcendentals=1 << 20),
        name="pre",
    )(pair, gain, bias, w_proj, w_gate)


def gate_kernel(pair, gain, bias, w_out_gate, out, held, affine, loaded, sems, held_sems):
    rows, cols, channels = held.shape
    small = copies([(gain, affine.at[0:1]), (bias, affine.at[1:2]), (w_out_gate, loaded)], sems)
    large = chunks(pair, held, held_sems)
    for copy in small + large:
        copy.start()
    for copy in small:
        copy.wait()
    for s in range(0, rows, STEP):
        large[s // STEP].wait()
        for t in range(s, s + STEP, 2):
            x = held[t : t + 2].reshape(2 * cols, channels).astype(jnp.float32)
            normed = normalized(x, affine[0:1], affine[1:2])
            gates = jnp.dot(normed, loaded[...], preferred_element_type=jnp.float32)
            out[t : t + 2] = sigmoid(gates).astype(jnp.bfloat16).reshape(2, cols, channels)


def gate(pair, gain, bias, w_out_gate):
    rows, cols, channels = pair.shape
    return pl.pallas_call(
        gate_kernel,
        in_specs=[pl.BlockSpec(memory_space=pl.ANY)] * 4,
        out_specs=pl.BlockSpec(memory_space=pltpu.VMEM),
        out_shape=jax.ShapeDtypeStruct((rows, cols, channels), jnp.bfloat16),
        scratch_shapes=[
            pltpu.VMEM((rows, cols, channels), jnp.bfloat16),
            pltpu.VMEM((2, channels), jnp.float32),
            pltpu.VMEM((channels, channels), jnp.bfloat16),
            pltpu.SemaphoreType.DMA((3,)),
            pltpu.SemaphoreType.DMA((rows // STEP,)),
        ],
        compiler_params=pltpu.CompilerParams(vmem_limit_bytes=NEARLY),
        cost_estimate=pl.CostEstimate(flops=1 << 30, bytes_accessed=16 << 20, transcendentals=1 << 20),
        name="gate",
    )(pair, gain, bias, w_out_gate)


def mid_kernel(core, chan, other, out, a_side, b_side):
    groups, rows, cols = other.shape
    across = 8
    mine = pl.multiple_of(core[0] * rows, rows)
    theirs = pl.multiple_of(rows - core[0] * rows, rows)
    for s, (r, q) in enumerate(PLACES):
        here = slice(q * cols, (q + 1) * cols)
        a_side[r * rows : (r + 1) * rows, here] = chan[s, 0]
        b_side[r, pl.ds(mine, rows), here] = chan[s, 1]
        b_side[r, pl.ds(theirs, rows), here] = other[s]
    for g in range(0, across, 2):
        b = b_side[g : g + 2].reshape(2 * cols, across * cols)
        m = lax.dot_general(a_side[...], b, NT, preferred_element_type=jnp.float32).astype(jnp.bfloat16)
        for r in range(groups // across):
            for h in range(2):
                out[PLACES.index((r, g + h))] = m[r * rows : (r + 1) * rows, h * cols : (h + 1) * cols]


def mid(core, chan, other):
    groups, rows, cols = other.shape
    return pl.pallas_call(
        mid_kernel,
        in_specs=[
            pl.BlockSpec(memory_space=pltpu.SMEM),
            pl.BlockSpec(memory_space=pltpu.VMEM),
            pl.BlockSpec(memory_space=pltpu.VMEM),
        ],
        out_specs=pl.BlockSpec(memory_space=pltpu.VMEM),
        out_shape=jax.ShapeDtypeStruct((groups, rows, cols), jnp.bfloat16),
        scratch_shapes=[
            pltpu.VMEM((8 * rows, 8 * cols), jnp.bfloat16),
            pltpu.VMEM((8, 2 * rows, 8 * cols), jnp.bfloat16),
        ],
        compiler_params=pltpu.CompilerParams(vmem_limit_bytes=VMEM),
        cost_estimate=pl.CostEstimate(flops=1 << 30, bytes_accessed=4 << 20, transcendentals=0),
        name="mid",
    )(core, chan, other)


def post_kernel(back, gates, gain, bias, w_out, out, made, loaded, wide, sem, out_sems):
    hidden, rows, cols = back.shape
    channels = loaded.shape[1]
    weight = pltpu.make_async_copy(w_out, loaded, sem)
    weight.start()
    wide[...] = jnp.zeros_like(wide)
    weight.wait()
    wide[:hidden, :channels] = loaded[...]
    wide[hidden:, channels:] = loaded[...]
    writes = chunks(made, out, out_sems)
    for s in range(0, rows, STEP):
        m = back[:, s : s + STEP, :].astype(jnp.float32)
        centered = m - jnp.sum(m, axis=0) * (1.0 / hidden)
        scale = lax.rsqrt(jnp.sum(centered * centered, axis=0) * (1.0 / hidden) + EPS)
        turned = []
        for c in range(0, hidden, 16):
            lead = jnp.stack([centered[c + d] * scale * gain[c + d] + bias[c + d] for d in range(16)], axis=0)
            turned.append(jnp.swapaxes(lead.astype(jnp.bfloat16), 0, 1))
        normed = jnp.concatenate(turned, axis=1)
        for t in range(0, STEP, 2):
            two = normed[t : t + 2].reshape(2 * hidden, cols)
            projected = lax.dot_general(two, wide[...], TN, preferred_element_type=jnp.float32)
            for h in range(2):
                mine = projected[:, h * channels : (h + 1) * channels]
                made[s + t + h] = (gates[s + t + h].astype(jnp.float32) * mine).astype(jnp.bfloat16)
        writes[s // STEP].start()
    for copy in writes:
        copy.wait()


def post(back, gates, gain, bias, w_out):
    hidden, rows, cols = back.shape
    channels = w_out.shape[1]
    whole = pl.BlockSpec(memory_space=pl.ANY)
    scalars = pl.BlockSpec(memory_space=pltpu.SMEM)
    return pl.pallas_call(
        post_kernel,
        in_specs=[pl.BlockSpec(memory_space=pltpu.VMEM)] * 2 + [scalars, scalars, whole],
        out_specs=whole,
        out_shape=jax.ShapeDtypeStruct((rows, cols, channels), jnp.bfloat16),
        scratch_shapes=[
            pltpu.VMEM((rows, cols, channels), jnp.bfloat16),
            pltpu.VMEM((hidden, channels), jnp.bfloat16),
            pltpu.VMEM((2 * hidden, 2 * channels), jnp.bfloat16),
            pltpu.SemaphoreType.DMA,
            pltpu.SemaphoreType.DMA((rows // STEP,)),
        ],
        compiler_params=pltpu.CompilerParams(vmem_limit_bytes=FEW),
        cost_estimate=pl.CostEstimate(flops=1 << 28, bytes_accessed=5 << 20, transcendentals=0),
        name="post",
    )(back, gates, gain, bias, w_out)


def local(pair, in_gain, in_bias, w_proj, w_gate, w_out_gate, out_gain, out_bias, w_out):
    gain, bias = in_gain.reshape(1, -1), in_bias.reshape(1, -1)
    lead = pre(pair, gain, bias, w_proj, w_gate)
    gates = gate(pair, gain, bias, w_out_gate)
    chan = lax.all_to_all(lead, CHIPS, 0, 0, tiled=True)
    chan, gates = lax.optimization_barrier((chan, gates))
    other = lax.ppermute(chan[:, 1], "core", [(0, 1), (1, 0)])
    core = lax.axis_index("core").astype(jnp.int32).reshape(1)
    back = lax.all_to_all(mid(core, chan, other), CHIPS, 0, 0, tiled=True)
    return post(back, gates, out_gain, out_bias, w_out)


def solution(mesh):
    fine = Mesh(mesh.devices.reshape(2, 4, 2, 2, 4), ("xh", "z", "core", "xl", "y"))
    place = P(("xh", "z", "core"), ("xl", "y"), None)
    return jax.shard_map(
        local,
        mesh=fine,
        in_specs=(place, P(), P(), P(), P(), P(), P(), P(), P()),
        out_specs=place,
        check_vma=False,
    )
```

```python
import jax
import jax.numpy as jnp
from jax import lax
from jax.experimental import pallas as pl
from jax.experimental.pallas import tpu as pltpu
from jax.sharding import Mesh
from jax.sharding import PartitionSpec as P

CHIPS = ("xh", "z", "y", "xl")
PLACES = [(xh * 4 + z, xl * 4 + y) for xh in range(2) for z in range(4) for y in range(4) for xl in range(2)]
STEP = 16
EPS = 1e-05
FEW = 24 << 20
VMEM = 48 << 20
NEARLY = 60 << 20
MOST = 58 << 20
NT = (((1,), (1,)), ((), ()))
TN = (((0,), (0,)), ((), ()))


def sigmoid(x):
    return 0.5 * jnp.tanh(0.5 * x) + 0.5


def normalized(x, gain, bias):
    share = 1.0 / x.shape[-1]
    centered = x - jnp.sum(x, axis=-1, keepdims=True) * share
    var = jnp.sum(centered * centered, axis=-1, keepdims=True) * share
    return (centered * lax.rsqrt(var + EPS) * gain + bias).astype(jnp.bfloat16)


def copies(pairs, sems):
    return [pltpu.make_async_copy(src, dst, sems.at[n]) for n, (src, dst) in enumerate(pairs)]


def chunks(source, target, sems):
    rows = target.shape[0]
    spans = [slice(s, s + STEP) for s in range(0, rows, STEP)]
    return copies([(source.at[span], target.at[span]) for span in spans], sems)


def pre_kernel(pair, gain, bias, w_proj, w_gate, out, held, made, affine, loaded, weights, gains, biases, sems, held_sems, out_sems):
    rows, cols, channels = held.shape
    hidden = channels // 2
    small = copies(
        [(gain, affine.at[0:1]), (bias, affine.at[1:2]), (w_proj, loaded.at[0]), (w_gate, loaded.at[1])], sems
    )
    large = chunks(pair, held, held_sems)
    for copy in small + large:
        copy.start()
    for copy in small:
        copy.wait()
    for n in range(2):
        half = loaded[n].astype(jnp.float32).T * 0.5
        weights[n * channels : (n + 1) * channels] = half.astype(jnp.bfloat16)
    gains[...] = jnp.broadcast_to(affine[0:1], (cols, channels)).T
    biases[...] = jnp.broadcast_to(affine[1:2], (cols, channels)).T

    def products(first):
        x = held[first : first + 2].reshape(2 * cols, channels).T.astype(jnp.float32)
        centered = x - jnp.sum(x, axis=0, keepdims=True) * (1.0 / channels)
        var = jnp.sum(centered * centered, axis=0, keepdims=True) * (1.0 / channels)
        x = centered * lax.rsqrt(var + EPS)
        normed = [x[:, h * cols : (h + 1) * cols] * gains[...] + biases[...] for h in range(2)]
        normed = jnp.concatenate(normed, axis=1).astype(jnp.bfloat16)
        both = jnp.dot(weights[...], normed, preferred_element_type=jnp.float32)
        return (jnp.tanh(both[channels:]) * both[:channels] + both[:channels]).astype(jnp.bfloat16)

    spans = [slice(s, s + STEP) for s in range(0, rows, STEP)]
    writes = copies([(made.at[:, :, span], out.at[:, :, span]) for span in spans], out_sems)
    for s in range(0, rows, STEP):
        large[s // STEP].wait()
        y = [products(s + t) for t in range(0, STEP, 2)]
        for c in range(0, channels, 16):
            lead = jnp.stack([v[c : c + 16, h * cols : (h + 1) * cols] for v in y for h in range(2)], axis=0)
            made[c % hidden : c % hidden + 16, c // hidden, s : s + STEP] = jnp.swapaxes(lead, 0, 1)
        writes[s // STEP].start()
    for copy in writes:
        copy.wait()


def pre(pair, gain, bias, w_proj, w_gate):
    rows, cols, channels = pair.shape
    hidden = channels // 2
    return pl.pallas_call(
        pre_kernel,
        in_specs=[pl.BlockSpec(memory_space=pl.ANY)] * 5,
        out_specs=pl.BlockSpec(memory_space=pl.ANY),
        out_shape=jax.ShapeDtypeStruct((hidden, 2, rows, cols), jnp.bfloat16),
        scratch_shapes=[
            pltpu.VMEM((rows, cols, channels), jnp.bfloat16),
            pltpu.VMEM((hidden, 2, rows, cols), jnp.bfloat16),
            pltpu.VMEM((2, channels), jnp.float32),
            pltpu.VMEM((2, channels, channels), jnp.bfloat16),
            pltpu.VMEM((2 * channels, channels), jnp.bfloat16),
            pltpu.VMEM((channels, cols), jnp.float32),
            pltpu.VMEM((channels, cols), jnp.float32),
            pltpu.SemaphoreType.DMA((4,)),
            pltpu.SemaphoreType.DMA((rows // STEP,)),
            pltpu.SemaphoreType.DMA((rows // STEP,)),
        ],
        compiler_params=pltpu.CompilerParams(vmem_limit_bytes=MOST),
        cost_estimate=pl.CostEstimate(flops=1 << 30, bytes_accessed=4 << 20, transcendentals=1 << 20),
        name="pre",
    )(pair, gain, bias, w_proj, w_gate)


def gate_kernel(pair, gain, bias, w_out_gate, out, held, affine, loaded, sems, held_sems):
    rows, cols, channels = held.shape
    small = copies([(gain, affine.at[0:1]), (bias, affine.at[1:2]), (w_out_gate, loaded)], sems)
    large = chunks(pair, held, held_sems)
    for copy in small + large:
        copy.start()
    for copy in small:
        copy.wait()
    for s in range(0, rows, STEP):
        large[s // STEP].wait()
        for t in range(s, s + STEP, 2):
            x = held[t : t + 2].reshape(2 * cols, channels).astype(jnp.float32)
            normed = normalized(x, affine[0:1], affine[1:2])
            gates = jnp.dot(normed, loaded[...], preferred_element_type=jnp.float32)
            out[t : t + 2] = sigmoid(gates).astype(jnp.bfloat16).reshape(2, cols, channels)


def gate(pair, gain, bias, w_out_gate):
    rows, cols, channels = pair.shape
    return pl.pallas_call(
        gate_kernel,
        in_specs=[pl.BlockSpec(memory_space=pl.ANY)] * 4,
        out_specs=pl.BlockSpec(memory_space=pltpu.VMEM),
        out_shape=jax.ShapeDtypeStruct((rows, cols, channels), jnp.bfloat16),
        scratch_shapes=[
            pltpu.VMEM((rows, cols, channels), jnp.bfloat16),
            pltpu.VMEM((2, channels), jnp.float32),
            pltpu.VMEM((channels, channels), jnp.bfloat16),
            pltpu.SemaphoreType.DMA((3,)),
            pltpu.SemaphoreType.DMA((rows // STEP,)),
        ],
        compiler_params=pltpu.CompilerParams(vmem_limit_bytes=NEARLY),
        cost_estimate=pl.CostEstimate(flops=1 << 30, bytes_accessed=16 << 20, transcendentals=1 << 20),
        name="gate",
    )(pair, gain, bias, w_out_gate)


def spread(a_side, b_side, side, put):
    cols = 128
    for n in range(0, b_side.shape[0], 2 * cols):
        b = b_side[n : n + 2 * cols]
        m = lax.dot_general(a_side[...], b, NT, preferred_element_type=jnp.float32)
        for h in range(2):
            block = m[:, h * cols : (h + 1) * cols]
            turned = pltpu.roll(block, cols // 2, 1)
            low = jnp.full(block.shape, side, jnp.int32) == 0
            g = (n + h * cols) // (cols // 2)
            put(g, jnp.where(low, block, turned))
            put(g + 1, jnp.where(low, turned, block))


def own_kernel(core, chan, a_side, out, b_side):
    rows, cols = chan.shape[2:]
    for s, (r, q) in enumerate(PLACES):
        here = slice(r * rows, (r + 1) * rows), slice(q * cols, (q + 1) * cols)
        a_side[here] = chan[s, 0]
        b_side[here] = chan[s, 1]

    def put(g, m):
        for r in range(8):
            out[PLACES.index((r, g))] = m[r * rows : (r + 1) * rows].astype(jnp.bfloat16)

    spread(a_side, b_side, core[0], put)


def own(core, chan):
    groups, _, rows, cols = chan.shape
    vmem = pl.BlockSpec(memory_space=pltpu.VMEM)
    return pl.pallas_call(
        own_kernel,
        in_specs=[pl.BlockSpec(memory_space=pltpu.SMEM), vmem],
        out_specs=[vmem, vmem],
        out_shape=[
            jax.ShapeDtypeStruct((8 * rows, 8 * cols), jnp.bfloat16),
            jax.ShapeDtypeStruct((groups, rows, cols), jnp.bfloat16),
        ],
        scratch_shapes=[pltpu.VMEM((8 * rows, 8 * cols), jnp.bfloat16)],
        compiler_params=pltpu.CompilerParams(vmem_limit_bytes=VMEM),
        cost_estimate=pl.CostEstimate(flops=1 << 29, bytes_accessed=4 << 20, transcendentals=0),
        name="own",
    )(core, chan)


def mid_kernel(core, a_side, mine, other, out, b_side):
    rows, cols = other.shape[1:]
    side = 1 - core[0]
    for s, (r, q) in enumerate(PLACES):
        b_side[r * rows : (r + 1) * rows, q * cols : (q + 1) * cols] = other[s]
    lanes = lax.broadcasted_iota(jnp.int32, (rows, cols), 1) // (cols // 2) == side

    def put(g, m):
        for r in range(8):
            s = PLACES.index((r, g))
            part = jnp.where(lanes, m[r * rows : (r + 1) * rows], mine[s].astype(jnp.float32))
            out[s] = part.astype(jnp.bfloat16)

    spread(a_side, b_side, side, put)


def mid(core, a_side, mine, other):
    groups, rows, cols = other.shape
    vmem = pl.BlockSpec(memory_space=pltpu.VMEM)
    return pl.pallas_call(
        mid_kernel,
        in_specs=[pl.BlockSpec(memory_space=pltpu.SMEM), vmem, vmem, vmem],
        out_specs=vmem,
        out_shape=jax.ShapeDtypeStruct((groups, rows, cols), jnp.bfloat16),
        scratch_shapes=[pltpu.VMEM((8 * rows, 8 * cols), jnp.bfloat16)],
        compiler_params=pltpu.CompilerParams(vmem_limit_bytes=VMEM),
        cost_estimate=pl.CostEstimate(flops=1 << 29, bytes_accessed=4 << 20, transcendentals=0),
        name="mid",
    )(core, a_side, mine, other)


def post_kernel(back, gates, gain, bias, w_out, out, made, loaded, wide, sem, out_sems):
    hidden, rows, cols = back.shape
    channels = loaded.shape[1]
    weight = pltpu.make_async_copy(w_out, loaded, sem)
    weight.start()
    ends = [*range(STEP, rows, STEP), rows - STEP // 2, rows]
    spans = [slice(first, end) for first, end in zip([0] + ends, ends)]
    writes = copies([(made.at[span], out.at[span]) for span in spans], out_sems)

    def mixed(s):
        m = back[:, s : s + STEP, :].astype(jnp.float32)
        centered = m - jnp.sum(m, axis=0) * (1.0 / hidden)
        scale = lax.rsqrt(jnp.sum(centered * centered, axis=0) * (1.0 / hidden) + EPS)
        turned = []
        for c in range(0, hidden, 16):
            lead = jnp.stack([centered[c + d] * scale * gain[c + d] + bias[c + d] for d in range(16)], axis=0)
            turned.append(jnp.swapaxes(lead.astype(jnp.bfloat16), 0, 1))
        return jnp.concatenate(turned, axis=1)

    normed = mixed(0)
    wide[...] = jnp.zeros_like(wide)
    weight.wait()
    wide[:hidden, :channels] = loaded[...]
    wide[hidden:, channels:] = loaded[...]
    for s in range(0, rows, STEP):
        later = mixed(s + STEP) if s + STEP < rows else None
        for t in range(0, STEP, 2):
            two = normed[t : t + 2].reshape(2 * hidden, cols)
            projected = lax.dot_general(two, wide[...], TN, preferred_element_type=jnp.float32)
            for h in range(2):
                mine = projected[:, h * channels : (h + 1) * channels]
                made[s + t + h] = (gates[s + t + h].astype(jnp.float32) * mine).astype(jnp.bfloat16)
            if s + t + 2 in ends:
                writes[ends.index(s + t + 2)].start()
        normed = later
    for copy in writes:
        copy.wait()


def post(back, gates, gain, bias, w_out):
    hidden, rows, cols = back.shape
    channels = w_out.shape[1]
    whole = pl.BlockSpec(memory_space=pl.ANY)
    scalars = pl.BlockSpec(memory_space=pltpu.SMEM)
    return pl.pallas_call(
        post_kernel,
        in_specs=[pl.BlockSpec(memory_space=pltpu.VMEM)] * 2 + [scalars, scalars, whole],
        out_specs=whole,
        out_shape=jax.ShapeDtypeStruct((rows, cols, channels), jnp.bfloat16),
        scratch_shapes=[
            pltpu.VMEM((rows, cols, channels), jnp.bfloat16),
            pltpu.VMEM((hidden, channels), jnp.bfloat16),
            pltpu.VMEM((2 * hidden, 2 * channels), jnp.bfloat16),
            pltpu.SemaphoreType.DMA,
            pltpu.SemaphoreType.DMA((rows // STEP + 1,)),
        ],
        compiler_params=pltpu.CompilerParams(vmem_limit_bytes=FEW),
        cost_estimate=pl.CostEstimate(flops=1 << 28, bytes_accessed=5 << 20, transcendentals=0),
        name="post",
    )(back, gates, gain, bias, w_out)


def local(pair, in_gain, in_bias, w_proj, w_gate, w_out_gate, out_gain, out_bias, w_out):
    gain, bias = in_gain.reshape(1, -1), in_bias.reshape(1, -1)
    lead = pre(pair, gain, bias, w_proj, w_gate)
    gates = gate(pair, gain, bias, w_out_gate)
    chan = lax.all_to_all(lead, CHIPS, 0, 0, tiled=True)
    chan, gates = lax.optimization_barrier((chan, gates))
    other = lax.ppermute(chan[:, 1], "core", [(0, 1), (1, 0)])
    core = lax.axis_index("core").astype(jnp.int32).reshape(1)
    back = lax.all_to_all(mid(core, *own(core, chan), other), CHIPS, 0, 0, tiled=True)
    return post(back, gates, out_gain, out_bias, w_out)


def solution(mesh):
    fine = Mesh(mesh.devices.reshape(2, 4, 2, 2, 4), ("xh", "z", "core", "xl", "y"))
    place = P(("xh", "z", "core"), ("xl", "y"), None)
    return jax.shard_map(
        local,
        mesh=fine,
        in_specs=(place, P(), P(), P(), P(), P(), P(), P(), P()),
        out_specs=place,
        check_vma=False,
    )
```

```python
import jax
import jax.numpy as jnp
from jax import lax
from jax.experimental import pallas as pl
from jax.experimental.pallas import tpu as pltpu
from jax.sharding import Mesh
from jax.sharding import PartitionSpec as P

CHIPS = ("xh", "z", "y", "xl")
PLACES = [(xh * 4 + z, xl * 4 + y) for xh in range(2) for z in range(4) for y in range(4) for xl in range(2)]
STEP = 16
EPS = 1e-05
FEW = 24 << 20
VMEM = 48 << 20
NEARLY = 60 << 20
MOST = 58 << 20
NT = (((1,), (1,)), ((), ()))
TN = (((0,), (0,)), ((), ()))


def sigmoid(x):
    return 0.5 * jnp.tanh(0.5 * x) + 0.5


def normalized(x, gain, bias):
    share = 1.0 / x.shape[-1]
    centered = x - jnp.sum(x, axis=-1, keepdims=True) * share
    var = jnp.sum(centered * centered, axis=-1, keepdims=True) * share
    return (centered * lax.rsqrt(var + EPS) * gain + bias).astype(jnp.bfloat16)


def copies(pairs, sems):
    return [pltpu.make_async_copy(src, dst, sems.at[n]) for n, (src, dst) in enumerate(pairs)]


def chunks(source, target, sems):
    rows = target.shape[0]
    spans = [slice(s, s + STEP) for s in range(0, rows, STEP)]
    return copies([(source.at[span], target.at[span]) for span in spans], sems)


def pre_kernel(pair, gain, bias, w_proj, w_gate, out, held, made, affine, loaded, weights, gains, biases, sems, held_sems, out_sems):
    rows, cols, channels = held.shape
    hidden = channels // 2
    small = copies(
        [(gain, affine.at[0:1]), (bias, affine.at[1:2]), (w_proj, loaded.at[0]), (w_gate, loaded.at[1])], sems
    )
    starts = [0, STEP]
    parts = [slice(first, end) for first, end in zip(starts, starts[1:] + [rows])]
    large = copies([(pair.at[part], held.at[part]) for part in parts], held_sems)
    for copy in small + large:
        copy.start()
    for copy in small:
        copy.wait()
    for n in range(2):
        half = loaded[n].astype(jnp.float32).T * 0.5
        weights[n * channels : (n + 1) * channels] = half.astype(jnp.bfloat16)
    gains[...] = jnp.broadcast_to(affine[0:1], (cols, channels)).T
    biases[...] = jnp.broadcast_to(affine[1:2], (cols, channels)).T

    def products(first):
        x = held[first : first + 2].reshape(2 * cols, channels).T.astype(jnp.float32)
        centered = x - jnp.sum(x, axis=0, keepdims=True) * (1.0 / channels)
        var = jnp.sum(centered * centered, axis=0, keepdims=True) * (1.0 / channels)
        x = centered * lax.rsqrt(var + EPS)
        normed = [x[:, h * cols : (h + 1) * cols] * gains[...] + biases[...] for h in range(2)]
        normed = jnp.concatenate(normed, axis=1).astype(jnp.bfloat16)
        both = jnp.dot(weights[...], normed, preferred_element_type=jnp.float32)
        return (jnp.tanh(both[channels:]) * both[:channels] + both[:channels]).astype(jnp.bfloat16)

    spans = [slice(s, s + STEP) for s in range(0, rows, STEP)]
    writes = copies([(made.at[:, :, span], out.at[:, :, span]) for span in spans], out_sems)
    for s in range(0, rows, STEP):
        if s in starts:
            large[starts.index(s)].wait()
        y = [products(s + t) for t in range(0, STEP, 2)]
        for c in range(0, channels, 16):
            lead = jnp.stack([v[c : c + 16, h * cols : (h + 1) * cols] for v in y for h in range(2)], axis=0)
            made[c % hidden : c % hidden + 16, c // hidden, s : s + STEP] = jnp.swapaxes(lead, 0, 1)
        writes[s // STEP].start()
    for copy in writes:
        copy.wait()


def pre(pair, gain, bias, w_proj, w_gate):
    rows, cols, channels = pair.shape
    hidden = channels // 2
    return pl.pallas_call(
        pre_kernel,
        in_specs=[pl.BlockSpec(memory_space=pl.ANY)] * 5,
        out_specs=pl.BlockSpec(memory_space=pl.ANY),
        out_shape=jax.ShapeDtypeStruct((hidden, 2, rows, cols), jnp.bfloat16),
        scratch_shapes=[
            pltpu.VMEM((rows, cols, channels), jnp.bfloat16),
            pltpu.VMEM((hidden, 2, rows, cols), jnp.bfloat16),
            pltpu.VMEM((2, channels), jnp.float32),
            pltpu.VMEM((2, channels, channels), jnp.bfloat16),
            pltpu.VMEM((2 * channels, channels), jnp.bfloat16),
            pltpu.VMEM((channels, cols), jnp.float32),
            pltpu.VMEM((channels, cols), jnp.float32),
            pltpu.SemaphoreType.DMA((4,)),
            pltpu.SemaphoreType.DMA((rows // STEP,)),
            pltpu.SemaphoreType.DMA((rows // STEP,)),
        ],
        compiler_params=pltpu.CompilerParams(vmem_limit_bytes=MOST),
        cost_estimate=pl.CostEstimate(flops=1 << 30, bytes_accessed=4 << 20, transcendentals=1 << 20),
        name="pre",
    )(pair, gain, bias, w_proj, w_gate)


def gate_kernel(pair, gain, bias, w_out_gate, out, held, affine, loaded, sems, held_sems):
    rows, cols, channels = held.shape
    small = copies([(gain, affine.at[0:1]), (bias, affine.at[1:2]), (w_out_gate, loaded)], sems)
    large = chunks(pair, held, held_sems)
    for copy in small + large:
        copy.start()
    for copy in small:
        copy.wait()
    for s in range(0, rows, STEP):
        large[s // STEP].wait()
        for t in range(s, s + STEP, 2):
            x = held[t : t + 2].reshape(2 * cols, channels).astype(jnp.float32)
            normed = normalized(x, affine[0:1], affine[1:2])
            gates = jnp.dot(normed, loaded[...], preferred_element_type=jnp.float32)
            out[t : t + 2] = sigmoid(gates).astype(jnp.bfloat16).reshape(2, cols, channels)


def gate(pair, gain, bias, w_out_gate):
    rows, cols, channels = pair.shape
    return pl.pallas_call(
        gate_kernel,
        in_specs=[pl.BlockSpec(memory_space=pl.ANY)] * 4,
        out_specs=pl.BlockSpec(memory_space=pltpu.VMEM),
        out_shape=jax.ShapeDtypeStruct((rows, cols, channels), jnp.bfloat16),
        scratch_shapes=[
            pltpu.VMEM((rows, cols, channels), jnp.bfloat16),
            pltpu.VMEM((2, channels), jnp.float32),
            pltpu.VMEM((channels, channels), jnp.bfloat16),
            pltpu.SemaphoreType.DMA((3,)),
            pltpu.SemaphoreType.DMA((rows // STEP,)),
        ],
        compiler_params=pltpu.CompilerParams(vmem_limit_bytes=NEARLY),
        cost_estimate=pl.CostEstimate(flops=1 << 30, bytes_accessed=16 << 20, transcendentals=1 << 20),
        name="gate",
    )(pair, gain, bias, w_out_gate)


def spread(a_side, b_side, side, put):
    cols = 128
    for n in range(0, b_side.shape[0], 2 * cols):
        b = b_side[n : n + 2 * cols]
        m = lax.dot_general(a_side[...], b, NT, preferred_element_type=jnp.float32)
        for h in range(2):
            block = m[:, h * cols : (h + 1) * cols]
            turned = pltpu.roll(block, cols // 2, 1)
            low = jnp.full(block.shape, side, jnp.int32) == 0
            g = (n + h * cols) // (cols // 2)
            put(g, jnp.where(low, block, turned))
            put(g + 1, jnp.where(low, turned, block))


def own_kernel(core, chan, a_side, out, b_side):
    rows, cols = chan.shape[2:]
    for s, (r, q) in enumerate(PLACES):
        here = slice(r * rows, (r + 1) * rows), slice(q * cols, (q + 1) * cols)
        a_side[here] = chan[s, 0]
        b_side[here] = chan[s, 1]

    def put(g, m):
        for r in range(8):
            out[PLACES.index((r, g))] = m[r * rows : (r + 1) * rows].astype(jnp.bfloat16)

    spread(a_side, b_side, core[0], put)


def own(core, chan):
    groups, _, rows, cols = chan.shape
    vmem = pl.BlockSpec(memory_space=pltpu.VMEM)
    return pl.pallas_call(
        own_kernel,
        in_specs=[pl.BlockSpec(memory_space=pltpu.SMEM), vmem],
        out_specs=[vmem, vmem],
        out_shape=[
            jax.ShapeDtypeStruct((8 * rows, 8 * cols), jnp.bfloat16),
            jax.ShapeDtypeStruct((groups, rows, cols), jnp.bfloat16),
        ],
        scratch_shapes=[pltpu.VMEM((8 * rows, 8 * cols), jnp.bfloat16)],
        compiler_params=pltpu.CompilerParams(vmem_limit_bytes=VMEM),
        cost_estimate=pl.CostEstimate(flops=1 << 29, bytes_accessed=4 << 20, transcendentals=0),
        name="own",
    )(core, chan)


def mid_kernel(core, a_side, mine, other, out, b_side):
    rows, cols = other.shape[1:]
    side = 1 - core[0]
    for s, (r, q) in enumerate(PLACES):
        b_side[r * rows : (r + 1) * rows, q * cols : (q + 1) * cols] = other[s]
    lanes = lax.broadcasted_iota(jnp.int32, (rows, cols), 1) // (cols // 2) == side

    def put(g, m):
        for r in range(8):
            s = PLACES.index((r, g))
            part = jnp.where(lanes, m[r * rows : (r + 1) * rows], mine[s].astype(jnp.float32))
            out[s] = part.astype(jnp.bfloat16)

    spread(a_side, b_side, side, put)


def mid(core, a_side, mine, other):
    groups, rows, cols = other.shape
    vmem = pl.BlockSpec(memory_space=pltpu.VMEM)
    return pl.pallas_call(
        mid_kernel,
        in_specs=[pl.BlockSpec(memory_space=pltpu.SMEM), vmem, vmem, vmem],
        out_specs=vmem,
        out_shape=jax.ShapeDtypeStruct((groups, rows, cols), jnp.bfloat16),
        scratch_shapes=[pltpu.VMEM((8 * rows, 8 * cols), jnp.bfloat16)],
        compiler_params=pltpu.CompilerParams(vmem_limit_bytes=VMEM),
        cost_estimate=pl.CostEstimate(flops=1 << 29, bytes_accessed=4 << 20, transcendentals=0),
        name="mid",
    )(core, a_side, mine, other)


def post_kernel(back, gates, gain, bias, w_out, out, made, loaded, wide, sem, out_sems):
    hidden, rows, cols = back.shape
    channels = loaded.shape[1]
    weight = pltpu.make_async_copy(w_out, loaded, sem)
    weight.start()
    ends = [*range(STEP, rows, STEP), rows - STEP // 2, rows]
    spans = [slice(first, end) for first, end in zip([0] + ends, ends)]
    writes = copies([(made.at[span], out.at[span]) for span in spans], out_sems)

    def mixed(s):
        m = back[:, s : s + STEP, :].astype(jnp.float32)
        centered = m - jnp.sum(m, axis=0) * (1.0 / hidden)
        scale = lax.rsqrt(jnp.sum(centered * centered, axis=0) * (1.0 / hidden) + EPS)
        turned = []
        for c in range(0, hidden, 16):
            lead = jnp.stack([centered[c + d] * scale * gain[c + d] + bias[c + d] for d in range(16)], axis=0)
            turned.append(jnp.swapaxes(lead.astype(jnp.bfloat16), 0, 1))
        return jnp.concatenate(turned, axis=1)

    normed = mixed(0)
    wide[...] = jnp.zeros_like(wide)
    weight.wait()
    wide[:hidden, :channels] = loaded[...]
    wide[hidden:, channels:] = loaded[...]
    for s in range(0, rows, STEP):
        later = mixed(s + STEP) if s + STEP < rows else None
        for t in range(0, STEP, 2):
            two = normed[t : t + 2].reshape(2 * hidden, cols)
            projected = lax.dot_general(two, wide[...], TN, preferred_element_type=jnp.float32)
            for h in range(2):
                mine = projected[:, h * channels : (h + 1) * channels]
                made[s + t + h] = (gates[s + t + h].astype(jnp.float32) * mine).astype(jnp.bfloat16)
            if s + t + 2 in ends:
                writes[ends.index(s + t + 2)].start()
        normed = later
    for copy in writes:
        copy.wait()


def post(back, gates, gain, bias, w_out):
    hidden, rows, cols = back.shape
    channels = w_out.shape[1]
    whole = pl.BlockSpec(memory_space=pl.ANY)
    scalars = pl.BlockSpec(memory_space=pltpu.SMEM)
    return pl.pallas_call(
        post_kernel,
        in_specs=[pl.BlockSpec(memory_space=pltpu.VMEM)] * 2 + [scalars, scalars, whole],
        out_specs=whole,
        out_shape=jax.ShapeDtypeStruct((rows, cols, channels), jnp.bfloat16),
        scratch_shapes=[
            pltpu.VMEM((rows, cols, channels), jnp.bfloat16),
            pltpu.VMEM((hidden, channels), jnp.bfloat16),
            pltpu.VMEM((2 * hidden, 2 * channels), jnp.bfloat16),
            pltpu.SemaphoreType.DMA,
            pltpu.SemaphoreType.DMA((rows // STEP + 1,)),
        ],
        compiler_params=pltpu.CompilerParams(vmem_limit_bytes=FEW),
        cost_estimate=pl.CostEstimate(flops=1 << 28, bytes_accessed=5 << 20, transcendentals=0),
        name="post",
    )(back, gates, gain, bias, w_out)


def local(pair, in_gain, in_bias, w_proj, w_gate, w_out_gate, out_gain, out_bias, w_out):
    gain, bias = in_gain.reshape(1, -1), in_bias.reshape(1, -1)
    lead = pre(pair, gain, bias, w_proj, w_gate)
    gates = gate(pair, gain, bias, w_out_gate)
    chan = lax.all_to_all(lead, CHIPS, 0, 0, tiled=True)
    chan, gates = lax.optimization_barrier((chan, gates))
    other = lax.ppermute(chan[:, 1], "core", [(0, 1), (1, 0)])
    core = lax.axis_index("core").astype(jnp.int32).reshape(1)
    back = lax.all_to_all(mid(core, *own(core, chan), other), CHIPS, 0, 0, tiled=True)
    return post(back, gates, out_gain, out_bias, w_out)


def solution(mesh):
    fine = Mesh(mesh.devices.reshape(2, 4, 2, 2, 4), ("xh", "z", "core", "xl", "y"))
    place = P(("xh", "z", "core"), ("xl", "y"), None)
    return jax.shard_map(
        local,
        mesh=fine,
        in_specs=(place, P(), P(), P(), P(), P(), P(), P(), P()),
        out_specs=place,
        check_vma=False,
    )
```
